32 devices in a mesh: groups: 2 (over y), adapter: 4 (over x, core), tensor: 4 (over z).
Axes of the slice: x: 2, y: 2, z: 4, core: 2. Of those that a mesh axis runs over, the one named last changes fastest.
Arguments:
- queries: bfloat16 [512, 8192], P(('groups', 'adapter'), 'tensor'), parts along dimension 0, may hold values from -6 to 6
- key_cache_rows: bfloat16 [512, 128, 1024], P(('groups', 'adapter'), None, 'tensor'), parts along dimension 0, may hold values from -6 to 6
- value_cache_rows: bfloat16 [512, 128, 1024], P(('groups', 'adapter'), None, 'tensor'), parts along dimension 0, may hold values from -6 to 6
- current_token_key: bfloat16 [512, 1024], P(('groups', 'adapter'), 'tensor'), parts along dimension 0, may hold values from -6 to 6
- current_token_value: bfloat16 [512, 1024], P(('groups', 'adapter'), 'tensor'), parts along dimension 0, may hold values from -6 to 6
- cache_valid_length: int32 [512], P(('groups', 'adapter')), parts along dimension 0, may hold values from 16 to 128, as said below
- request_adapter_index: int32 [512], P(('groups', 'adapter')), parts along dimension 0, may hold values from 0 to 31, as said below
- adapter_storage_slot: int32 [64], P('groups'), parts along dimension 0, may hold values from 0 to 31, as said below
- output_projection: bfloat16 [8192, 4096], P('tensor'), may hold values from -0.1875 to 0.1875
- adapter_down_weight: bfloat16 [32, 64, 8192], P('adapter', None, 'tensor'), may hold values from -0.25 to 0.25
- adapter_up_weight: bfloat16 [32, 64, 4096], P('adapter', None, 'tensor'), may hold values from -0.75 to 0.75
Outputs:
- layer_out: bfloat16 [512, 4096], P(('groups', 'adapter'), 'tensor'), parts along dimension 0
The draws below stay inside these ranges and needn't reach their ends.
There are 2 independent parts, one for each index of `groups`. The reference program is written for one: setup_inputs(seed, part) draws one part's arguments, and reference() takes and returns one part's arrays. A program takes and returns all parts, laid end to end along the dimension named above; an argument that names none is the same for every part. Nothing has to cross between parts.
Inputs may be any that keep to these rules, and one draw needn't show every extreme that they name: `request_adapter_index`: of the requests of one adapter index, at most 32 use adapters whose slots lie at any one adapter index (slot // 8); some adapter index serves exactly 32 from every adapter index. `adapter_storage_slot`: A permutation: every slot holds one adapter. `cache_valid_length`: the first request of every adapter index has all 128 positions valid.
All inputs are finite; a program needn't handle non-finite values.
Results may differ from the reference program's by a relative error of at most 0.008.
Values may be sent and summed in bfloat16 or wider, within the bound.
A program may use at most 128 MiB of HBM per device.

```python
import jax
import jax.numpy as jnp
from jax import lax

QUERY_HEADS = 64
KV_HEADS = 8
HEAD_WIDTH = 128
OUTPUT_FEATURES = 4096
ADAPTER_RANK = 64
REQ_DEV = 64
CTX = 128
ADAPT_DEV = 8
REQUESTS = 256
ADAPTER_TOTAL = 32
N_ADAPTER = 4


def routing(key):
    base_key = jax.random.fold_in(key, 11)
    perm_key, hot_key, pick_key, order_key, local_key = jax.random.split(base_key, 5)
    storage = jax.random.permutation(perm_key, ADAPTER_TOTAL).astype(jnp.int32)
    capacity = 2 * REQ_DEV // N_ADAPTER
    slots_all = N_ADAPTER * capacity
    hottest = jax.random.randint(hot_key, (), 0, N_ADAPTER)
    index = jnp.arange(slots_all, dtype=jnp.int32)
    noise = jax.random.randint(pick_key, (N_ADAPTER, slots_all), 1, 2 ** 20)
    is_hot = index // capacity == hottest
    ranking = jnp.where(is_hot[None, :], index[None, :], noise * slots_all + index[None, :])
    chosen = jnp.argsort(ranking, axis=1, stable=True)[:, :REQ_DEV]
    holders = chosen // capacity
    shuffle = jax.random.randint(order_key, (N_ADAPTER, REQ_DEV), 0, 2 ** 20) * REQ_DEV + jnp.arange(REQ_DEV, dtype=jnp.int32)[None, :]
    order = jnp.argsort(shuffle, axis=1, stable=True)
    holders = jnp.take_along_axis(holders, order, axis=1).reshape(-1)
    chosen_local = jax.random.randint(local_key, (N_ADAPTER * REQ_DEV,), 0, ADAPT_DEV)
    wanted = holders * ADAPT_DEV + chosen_local
    inverse = jnp.argsort(storage, stable=True).astype(jnp.int32)
    return (storage, jnp.take(inverse, wanted).astype(jnp.int32))


def draw_request_adapter_index(key, part):
    return routing(key)[1]


def draw_adapter_storage_slot(key, part):
    return routing(key)[0]


def draw_cache_valid_length(key, part):
    key = jax.random.fold_in(key, 5)
    lengths = jax.random.randint(key, (REQUESTS,), CTX // 8, CTX + 1)
    leading = jnp.arange(REQUESTS, dtype=jnp.int32) % REQ_DEV == 0
    return jnp.where(leading, CTX, lengths).astype(jnp.int32)


def draw_queries(key, part):
    key = jax.random.fold_in(key, 3)
    per_group = QUERY_HEADS // KV_HEADS
    values = jnp.clip(jax.random.normal(key, (REQUESTS, KV_HEADS, per_group, HEAD_WIDTH), jnp.float32), -6.0, 6.0)
    return values.reshape(REQUESTS, QUERY_HEADS * HEAD_WIDTH).astype(jnp.bfloat16)


def draw_key_cache_rows(key, part):
    key = jax.random.fold_in(key, 7)
    values = jnp.clip(jax.random.normal(key, (REQUESTS, CTX, KV_HEADS, HEAD_WIDTH), jnp.float32), -6.0, 6.0)
    return values.reshape(REQUESTS, CTX, KV_HEADS * HEAD_WIDTH).astype(jnp.bfloat16)


def block_scale(stream_key, extent, pieces, low, top_value):
    level = 1.0
    for position, blocks in pieces:
        steps = jax.random.uniform(jax.random.fold_in(jax.random.fold_in(stream_key, 6), position), (blocks,), jnp.float32, low / len(pieces), top_value / len(pieces))
        level = level * jnp.repeat(jnp.exp(steps), extent[position] // blocks).reshape((-1,) + (1,) * (len(extent) - 1 - position))
    return level


def normal_values(key, shape, spread, limit, shards=(), kind=jnp.bfloat16):
    factor_of = block_scale(key, shape, shards, -0.22, 0.18) if shards else 1.0
    result = jax.random.normal(key, shape, jnp.float32) * spread * factor_of
    return jnp.minimum(jnp.maximum(result, -limit), limit).astype(kind)


def setup_inputs(seed: int = 0, part: int = 0) -> dict:
    keys = jax.random.split(jax.random.key(seed), 12)
    part_splits = jax.random.split(jax.random.fold_in(keys[11], part), 12)
    return {
        "queries": draw_queries(jax.random.fold_in(jax.random.fold_in(keys[11], part), 71), part),
        "key_cache_rows": draw_key_cache_rows(jax.random.fold_in(jax.random.fold_in(keys[11], part), 71), part),
        "value_cache_rows": normal_values(part_splits[2], (REQUESTS, CTX, KV_HEADS * HEAD_WIDTH), 1.0, 6.0, ((0, 4), (2, 4))),
        "current_token_key": normal_values(part_splits[3], (REQUESTS, KV_HEADS * HEAD_WIDTH), 1.0, 6.0, ((0, 4), (1, 4))),
        "current_token_value": normal_values(part_splits[4], (REQUESTS, KV_HEADS * HEAD_WIDTH), 1.0, 6.0, ((0, 4), (1, 4))),
        "cache_valid_length": draw_cache_valid_length(jax.random.fold_in(jax.random.fold_in(keys[11], part), 71), part),
        "request_adapter_index": draw_request_adapter_index(jax.random.fold_in(jax.random.fold_in(keys[11], part), 71), part),
        "adapter_storage_slot": draw_adapter_storage_slot(jax.random.fold_in(jax.random.fold_in(keys[11], part), 71), part),
        "output_projection": normal_values(keys[8], (QUERY_HEADS * HEAD_WIDTH, OUTPUT_FEATURES), (QUERY_HEADS * HEAD_WIDTH // 8) ** -0.5, 0.1875, ((0, 4),)),
        "adapter_down_weight": normal_values(keys[9], (ADAPTER_TOTAL, ADAPTER_RANK, QUERY_HEADS * HEAD_WIDTH), (QUERY_HEADS * HEAD_WIDTH // 16) ** -0.5, 0.25, ((0, 4), (2, 4))),
        "adapter_up_weight": normal_values(keys[10], (ADAPTER_TOTAL, ADAPTER_RANK, OUTPUT_FEATURES), ADAPTER_RANK ** -0.5, 0.75, ((0, 4), (2, 4))),
    }


def reference(queries, key_cache_rows, value_cache_rows, current_token_key, current_token_value, cache_valid_length, request_adapter_index, adapter_storage_slot, output_projection, adapter_down_weight, adapter_up_weight):
    per_group = QUERY_HEADS // KV_HEADS
    scaling = HEAD_WIDTH ** -0.5
    query_all = queries.astype(jnp.float32).reshape(REQUESTS, KV_HEADS, per_group, HEAD_WIDTH)
    keys_all = key_cache_rows.astype(jnp.float32).reshape(REQUESTS, CTX, KV_HEADS, HEAD_WIDTH)
    values_all = value_cache_rows.astype(jnp.float32).reshape(REQUESTS, CTX, KV_HEADS, HEAD_WIDTH)
    fresh_key = current_token_key.astype(jnp.float32).reshape(REQUESTS, KV_HEADS, HEAD_WIDTH)
    fresh_value = current_token_value.astype(jnp.float32).reshape(REQUESTS, KV_HEADS, 1, HEAD_WIDTH)
    scores = jnp.einsum("rkgd,rpkd->rkgp", query_all, keys_all) * scaling
    fresh = jnp.einsum("rkgd,rkd->rkg", query_all, fresh_key) * scaling
    positions = jnp.arange(CTX, dtype=jnp.int32)
    usable = positions[None, :] < cache_valid_length[:, None]
    scores = jnp.where(usable[:, None, None, :], scores, -jnp.inf)
    largest = jnp.maximum(jnp.max(scores, axis=-1), fresh)
    weights = jnp.exp(scores - largest[..., None])
    self_weight = jnp.exp(fresh - largest)
    totals = jnp.sum(weights, axis=-1) + self_weight
    chances = (weights / totals[..., None]).astype(jnp.bfloat16)
    self_chance = (self_weight / totals).astype(jnp.bfloat16)
    blended = jnp.einsum("rkgp,rpkd->rkgd", chances.astype(jnp.float32), values_all)
    blended = blended + self_chance.astype(jnp.float32)[..., None] * fresh_value
    attended = blended.reshape(REQUESTS, QUERY_HEADS * HEAD_WIDTH).astype(jnp.bfloat16)
    projected = jnp.dot(attended, output_projection, preferred_element_type=jnp.float32)
    storage = jnp.take(adapter_storage_slot, request_adapter_index).astype(jnp.int32)

    def through_adapter(request_pair):
        request_row, request_storage_slot = request_pair
        down_weight_rows = adapter_down_weight[request_storage_slot]
        reduced_rank_state = jnp.dot(down_weight_rows, request_row, preferred_element_type=jnp.float32).astype(jnp.bfloat16)
        return jnp.dot(reduced_rank_state, adapter_up_weight[request_storage_slot], preferred_element_type=jnp.float32).astype(jnp.bfloat16)

    adapted = lax.map(through_adapter, (attended, storage))
    return (projected + adapted.astype(jnp.float32)).astype(jnp.bfloat16)
```

```python
import functools

import jax
import jax.numpy as jnp
from jax import lax
from jax.experimental import pallas as pl
from jax.experimental.pallas import tpu as pltpu
from jax.sharding import PartitionSpec as P

QUERY_HEADS = 64
KV_HEADS = 8
HEAD_WIDTH = 128
CHUNK = 8
MESH = pl.DeviceIdType.MESH
F32 = jnp.float32
BF16 = jnp.bfloat16


def offsets_of(n):
    return sorted(range(1, n), key=lambda o: (abs(o - n / 2), o))


def dot(a, b, dims=((1,), (0,))):
    return lax.dot_general(a, b, (dims, ((), ())), preferred_element_type=F32)


def kernel(
    n_a,
    n_t,
    cap,
    q_hbm,
    k_hbm,
    v_hbm,
    kc_hbm,
    vc_hbm,
    len_ref,
    id_ref,
    slot_ref,
    w_hbm,
    down_hbm,
    up_hbm,
    out_ref,
    q_v,
    k_v,
    v_v,
    kc_v,
    vc_v,
    w_v,
    down_v,
    up_v,
    qs,
    att,
    kcf,
    vcf,
    slot_v,
    rows_a,
    part_send,
    part_recv,
    row_send,
    row_recv,
    low_send,
    low_recv,
    back_send,
    back_recv,
    in_sem,
    k_sem,
    v_sem,
    w_sem,
    ps_sem,
    pr_sem,
    rs_sem,
    rr_sem,
    ls_sem,
    lr_sem,
    bs_sem,
    br_sem,
):
    g, a, t = lax.axis_index("groups"), lax.axis_index("adapter"), lax.axis_index("tensor")
    reqs, width = q_v.shape
    span = k_v.shape[1]
    heads = width // HEAD_WIDTH
    kv = kc_v.shape[1] // HEAD_WIDTH
    per = heads // kv
    residents, rank, _ = down_v.shape
    wide = residents * rank
    out_w = w_v.shape[2]
    packed = n_a * cap
    scaling = HEAD_WIDTH ** (-0.5)
    t_order = offsets_of(n_t)

    def on_t(offset):
        return (g, a, lax.rem(t + offset, n_t))

    def on_a(offset):
        return (g, lax.rem(a + offset, n_a), t)

    small = [
        pltpu.make_async_copy(q_hbm, q_v, in_sem.at[0]),
        pltpu.make_async_copy(kc_hbm, kc_v, in_sem.at[1]),
        pltpu.make_async_copy(vc_hbm, vc_v, in_sem.at[2]),
    ]
    down_copy = pltpu.make_async_copy(down_hbm, down_v, in_sem.at[3])
    up_copy = pltpu.make_async_copy(up_hbm, up_v, in_sem.at[4])

    def cache_copies(i):
        part = pl.ds(pl.multiple_of(i * CHUNK, CHUNK), CHUNK)
        return (
            pltpu.make_async_copy(k_hbm.at[part], k_v.at[part], k_sem.at[i]),
            pltpu.make_async_copy(v_hbm.at[part], v_v.at[part], v_sem.at[i]),
        )

    for copy in small:
        copy.start()
    for i in range(reqs // CHUNK):
        for copy in cache_copies(i):
            copy.start()
    w_copies = []
    for s, offset in enumerate(t_order + [0]):
        owner = lax.rem(t + offset, n_t)
        columns = pl.ds(pl.multiple_of(owner * out_w, 128), out_w)
        w_copies.append(pltpu.make_async_copy(w_hbm.at[:, columns], w_v.at[s], w_sem.at[s]))
    for copy in w_copies[:2]:
        copy.start()
    down_copy.start()
    for copy in w_copies[2:]:
        copy.start()
    up_copy.start()

    barrier = pltpu.get_barrier_semaphore()
    for offset in range(1, n_a):
        pl.semaphore_signal(barrier, inc=1, device_id=on_a(offset), device_id_type=MESH)
    for offset in range(1, n_t):
        pl.semaphore_signal(barrier, inc=1, device_id=on_t(offset), device_id_type=MESH)

    for r in range(reqs):
        slot_v[pl.ds(r, 1), :] = jnp.full((1, 128), slot_ref[id_ref[r]], jnp.int32)
    storage = slot_v[...]
    lane = lax.broadcasted_iota(jnp.int32, (reqs, 128), 1)
    holder = storage // residents
    local = storage - holder * residents
    local_hot = (local == lane).astype(F32).astype(BF16)
    away = holder - a
    away = jnp.where(away < 0, away + n_a, away)
    to_hot = away == lane
    before = lax.broadcasted_iota(jnp.int32, (reqs, reqs), 1) < lax.broadcasted_iota(
        jnp.int32, (reqs, reqs), 0
    )
    ranks = dot(before.astype(F32).astype(BF16), to_hot.astype(F32).astype(BF16))
    place = jnp.sum(jnp.where(to_hot, ranks, 0.0), axis=1, keepdims=True).astype(jnp.int32)
    place = place + away[:, :1] * cap
    packing = (
        (place == lax.broadcasted_iota(jnp.int32, (reqs, packed), 1)).astype(F32).astype(BF16)
    )

    for copy in small:
        copy.wait()
    for h in range(heads):
        qs[pl.ds(h, reqs, stride=heads), :] = q_v[
            :, h * HEAD_WIDTH : (h + 1) * HEAD_WIDTH
        ].astype(F32)
    kcf[...] = kc_v[...].astype(F32)
    vcf[...] = vc_v[...].astype(F32)

    def spread(block):
        return jnp.concatenate(
            [
                jnp.broadcast_to(
                    block[j : j + 1, c * HEAD_WIDTH : (c + 1) * HEAD_WIDTH], (per, HEAD_WIDTH)
                )
                for j in range(CHUNK)
                for c in range(kv)
            ],
            axis=0,
        )

    def attend(i, carry):
        k_copy, v_copy = cache_copies(i)
        rows = pl.ds(pl.multiple_of(i * (CHUNK * heads), CHUNK * heads), CHUNK * heads)
        part = pl.ds(pl.multiple_of(i * CHUNK, CHUNK), CHUNK)
        q_f = qs[rows, :]
        row_kv = lax.broadcasted_iota(jnp.int32, (heads, HEAD_WIDTH), 0) // per
        position = lax.broadcasted_iota(jnp.int32, (heads, span), 1)
        fresh = jnp.sum(q_f * spread(kcf[part, :]), axis=1, keepdims=True) * scaling
        k_copy.wait()
        scores = []
        for j in range(CHUNK):
            mine = q_f[j * heads : (j + 1) * heads]
            diag = jnp.concatenate(
                [jnp.where(row_kv == c, mine, 0.0) for c in range(kv)], axis=1
            ).astype(BF16)
            score = dot(diag, k_v[i * CHUNK + j], ((1,), (1,))) * scaling
            scores.append(jnp.where(position < len_ref[i * CHUNK + j], score, -jnp.inf))
        scores = jnp.concatenate(scores, axis=0)
        largest = jnp.maximum(jnp.max(scores, axis=1, keepdims=True), fresh)
        weights = jnp.exp(scores - largest)
        self_weight = jnp.exp(fresh - largest)
        total = jnp.sum(weights, axis=1, keepdims=True) + self_weight
        chances = (weights / total).astype(BF16)
        self_chance = (self_weight / total).astype(BF16).astype(F32)
        v_copy.wait()
        blended = []
        for j in range(CHUNK):
            both = dot(chances[j * heads : (j + 1) * heads], v_v[i * CHUNK + j])
            for c in range(kv):
                blended.append(
                    both[c * per : (c + 1) * per, c * HEAD_WIDTH : (c + 1) * HEAD_WIDTH]
                )
        blended = jnp.concatenate(blended, axis=0) + self_chance * spread(vcf[part, :])
        att[rows, :] = blended
        return carry

    lax.fori_loop(0, reqs // CHUNK, attend, 0)

    for h in range(heads):
        rows_a[:, h * HEAD_WIDTH : (h + 1) * HEAD_WIDTH] = att[
            pl.ds(h, reqs, stride=heads), :
        ].astype(BF16)

    pl.semaphore_wait(barrier, n_a - 1 + n_t - 1)

    step = 512
    for c in range(0, width, step):
        block = dot(packing, rows_a[:, c : c + step], ((0,), (0,))).astype(BF16)
        block = block.reshape(n_a, cap, step)
        row_send[:, :, c : c + step] = block
    row_send[:, :, width:] = (
        dot(packing, local_hot, ((0,), (0,))).astype(BF16).reshape(n_a, cap, 128)
    )
    row_copies = []
    for offset in range(1, n_a):
        copy = pltpu.make_async_remote_copy(
            src_ref=row_send.at[offset],
            dst_ref=row_recv.at[offset],
            send_sem=rs_sem.at[offset],
            recv_sem=rr_sem.at[offset],
            device_id=on_a(offset),
            device_id_type=MESH,
        )
        copy.start()
        row_copies.append(copy)

    part_copies = []

    def project(s, offset):
        w_copies[s].wait()
        half = out_w // 2
        for c in range(0, out_w, half):
            part_send[s, :, c : c + half] = dot(rows_a[...], w_v[s, :, c : c + half]).astype(BF16)
        copy = pltpu.make_async_remote_copy(
            src_ref=part_send.at[s],
            dst_ref=part_recv.at[s],
            send_sem=ps_sem.at[s],
            recv_sem=pr_sem.at[s],
            device_id=on_t(offset),
            device_id_type=MESH,
        )
        copy.start()
        part_copies.append(copy)

    for s, offset in enumerate(t_order):
        project(s, offset)

    down_copy.wait()
    for copy in row_copies:
        copy.wait()
    got = jnp.concatenate([row_send[0][None], row_recv[1:]], axis=0).reshape(packed, width + 128)
    expand = (
        lax.broadcasted_iota(jnp.int32, (128, wide), 1) // rank
        == lax.broadcasted_iota(jnp.int32, (128, wide), 0)
    )
    chosen = dot(got[:, width:], expand.astype(F32).astype(BF16)) > 0.5
    low = dot(got[:, :width], down_v[...].reshape(wide, width), ((1,), (1,)))
    low = jnp.where(chosen, low, 0.0)
    fold = low[:, :128]
    for c in range(128, wide, 128):
        fold = fold + low[:, c : c + 128]
    fold = fold + pltpu.roll(fold, rank, 1)
    left = lax.broadcasted_iota(jnp.int32, (packed // 2, 128), 1) < rank
    own_low = jnp.where(left, fold[: packed // 2], fold[packed // 2 :])
    low_send[...] = own_low.astype(BF16)
    low_copies = []
    for offset in t_order:
        copy = pltpu.make_async_remote_copy(
            src_ref=low_send,
            dst_ref=low_recv.at[offset],
            send_sem=ls_sem.at[offset],
            recv_sem=lr_sem.at[offset],
            device_id=on_t(offset),
            device_id_type=MESH,
        )
        copy.start()
        low_copies.append(copy)

    w_copies[n_t - 1].wait()
    share = dot(rows_a[...], w_v[n_t - 1])

    up_copy.wait()
    for copy in low_copies:
        copy.wait()
    for offset in t_order:
        own_low = own_low + low_recv[offset].astype(F32)
    turned = pltpu.roll(own_low, rank, 1)
    reduced = jnp.concatenate(
        [jnp.where(left, own_low, turned), jnp.where(left, turned, own_low)], axis=0
    )
    reduced = jnp.concatenate([reduced] * (wide // 128), axis=1)
    reduced = jnp.where(chosen, reduced, 0.0).astype(BF16)
    raised = dot(reduced, up_v[...].reshape(wide, out_w)).astype(BF16)
    back_send[...] = raised.reshape(n_a, cap, out_w)
    back_copies = []
    for offset in range(1, n_a):
        copy = pltpu.make_async_remote_copy(
            src_ref=back_send.at[offset],
            dst_ref=back_recv.at[offset],
            send_sem=bs_sem.at[offset],
            recv_sem=br_sem.at[offset],
            device_id=on_a(n_a - offset),
            device_id_type=MESH,
        )
        copy.start()
        back_copies.append(copy)

    for s, copy in enumerate(part_copies):
        copy.wait()
        share = share + part_recv[s].astype(F32)
    for copy in back_copies:
        copy.wait()
    came = jnp.concatenate([back_send[0][None], back_recv[1:]], axis=0).reshape(packed, out_w)
    out_ref[...] = (share + dot(packing, came)).astype(BF16)


def body(n_a, n_t, *operands):
    q, k, v, kc, vc, _, _, _, w, down, up = operands
    reqs, width = q.shape
    out_w = w.shape[1] // n_t
    cap = max(16, 2 * reqs // n_a)
    packed = n_a * cap
    heads = width // HEAD_WIDTH
    chunks = reqs // CHUNK
    dma = pltpu.SemaphoreType.DMA
    hbm = pl.BlockSpec(memory_space=pl.ANY)
    smem = pl.BlockSpec(memory_space=pltpu.SMEM)
    vmem = pltpu.VMEM
    return pl.pallas_call(
        functools.partial(kernel, n_a, n_t, cap),
        out_shape=jax.ShapeDtypeStruct((reqs, out_w), BF16),
        in_specs=[hbm] * 5 + [smem] * 3 + [hbm] * 3,
        out_specs=pl.BlockSpec(memory_space=pltpu.VMEM),
        scratch_shapes=[
            vmem(q.shape, BF16),
            vmem(k.shape, BF16),
            vmem(v.shape, BF16),
            vmem(kc.shape, BF16),
            vmem(vc.shape, BF16),
            vmem((n_t, width, out_w), BF16),
            vmem(down.shape, BF16),
            vmem(up.shape, BF16),
            vmem((reqs * heads, HEAD_WIDTH), F32),
            vmem((reqs * heads, HEAD_WIDTH), F32),
            vmem(kc.shape, F32),
            vmem(vc.shape, F32),
            vmem((reqs, 128), jnp.int32),
            vmem((reqs, width), BF16),
            vmem((n_t - 1, reqs, out_w), BF16),
            vmem((n_t - 1, reqs, out_w), BF16),
            vmem((n_a, cap, width + 128), BF16),
            vmem((n_a, cap, width + 128), BF16),
            vmem((packed // 2, 128), BF16),
            vmem((n_t, packed // 2, 128), BF16),
            vmem((n_a, cap, out_w), BF16),
            vmem((n_a, cap, out_w), BF16),
            dma((5,)),
            dma((chunks,)),
            dma((chunks,)),
            dma((n_t,)),
            dma((n_t,)),
            dma((n_t,)),
            dma((n_a,)),
            dma((n_a,)),
            dma((n_t,)),
            dma((n_t,)),
            dma((n_a,)),
            dma((n_a,)),
        ],
        compiler_params=pltpu.CompilerParams(
            collective_id=0, has_side_effects=True, vmem_limit_bytes=56 * 1024 * 1024
        ),
    )(*operands)


def solution(mesh):
    in_specs = (
        P(("groups", "adapter"), "tensor"),
        P(("groups", "adapter"), None, "tensor"),
        P(("groups", "adapter"), None, "tensor"),
        P(("groups", "adapter"), "tensor"),
        P(("groups", "adapter"), "tensor"),
        P(("groups", "adapter")),
        P(("groups", "adapter")),
        P("groups"),
        P("tensor", None),
        P("adapter", None, "tensor"),
        P("adapter", None, "tensor"),
    )
    out_specs = P(("groups", "adapter"), "tensor")
    run = functools.partial(body, mesh.shape["adapter"], mesh.shape["tensor"])
    return jax.shard_map(run, mesh=mesh, in_specs=in_specs, out_specs=out_specs, check_vma=False)
```

```python
import functools

import jax
import jax.numpy as jnp
from jax import lax
from jax.experimental import pallas as pl
from jax.experimental.pallas import tpu as pltpu
from jax.sharding import PartitionSpec as P

QUERY_HEADS = 64
KV_HEADS = 8
HEAD_WIDTH = 128
CHUNK = 32
MESH = pl.DeviceIdType.MESH
F32 = jnp.float32
BF16 = jnp.bfloat16


def offsets_of(n):
    return sorted(range(1, n), key=lambda o: (abs(o - n / 2), o))


def dot(a, b, dims=((1,), (0,))):
    return lax.dot_general(a, b, (dims, ((), ())), preferred_element_type=F32)


def kernel(
    n_a,
    n_t,
    cap,
    q_hbm,
    k_hbm,
    v_hbm,
    kc_hbm,
    vc_hbm,
    len_ref,
    id_ref,
    slot_ref,
    w_hbm,
    down_hbm,
    up_hbm,
    out_ref,
    q_v,
    k_v,
    v_v,
    kc_v,
    vc_v,
    w_v,
    down_v,
    up_v,
    qs,
    att,
    kcf,
    vcf,
    slot_v,
    rows_a,
    part_send,
    part_recv,
    row_send,
    row_recv,
    low_send,
    low_recv,
    back_send,
    back_recv,
    in_sem,
    k_sem,
    v_sem,
    w_sem,
    ps_sem,
    pr_sem,
    rs_sem,
    rr_sem,
    ls_sem,
    lr_sem,
    bs_sem,
    br_sem,
):
    g, a, t = lax.axis_index("groups"), lax.axis_index("adapter"), lax.axis_index("tensor")
    reqs, width = q_v.shape
    span = k_v.shape[1]
    heads = width // HEAD_WIDTH
    kv = kc_v.shape[1] // HEAD_WIDTH
    per = heads // kv
    residents, rank, _ = down_v.shape
    wide = residents * rank
    out_w = w_v.shape[2]
    packed = n_a * cap
    scaling = HEAD_WIDTH ** (-0.5)
    t_order = offsets_of(n_t)

    def on_t(offset):
        return (g, a, lax.rem(t + offset, n_t))

    def on_a(offset):
        return (g, lax.rem(a + offset, n_a), t)

    barrier = pltpu.get_barrier_semaphore()
    for offset in range(1, n_a):
        pl.semaphore_signal(barrier, inc=1, device_id=on_a(offset), device_id_type=MESH)
    for offset in range(1, n_t):
        pl.semaphore_signal(barrier, inc=1, device_id=on_t(offset), device_id_type=MESH)

    small = [
        pltpu.make_async_copy(q_hbm, q_v, in_sem.at[0]),
        pltpu.make_async_copy(kc_hbm, kc_v, in_sem.at[1]),
        pltpu.make_async_copy(vc_hbm, vc_v, in_sem.at[2]),
    ]
    down_copy = pltpu.make_async_copy(down_hbm, down_v, in_sem.at[3])
    up_copy = pltpu.make_async_copy(up_hbm, up_v, in_sem.at[4])

    def cache_copies(i):
        part = pl.ds(pl.multiple_of(i * CHUNK, CHUNK), CHUNK)
        return (
            pltpu.make_async_copy(k_hbm.at[part], k_v.at[part], k_sem.at[i]),
            pltpu.make_async_copy(v_hbm.at[part], v_v.at[part], v_sem.at[i]),
        )

    for copy in small:
        copy.start()
    for i in range(reqs // CHUNK):
        for copy in cache_copies(i):
            copy.start()
    w_copies = []
    for s, offset in enumerate(t_order + [0]):
        owner = lax.rem(t + offset, n_t)
        columns = pl.ds(pl.multiple_of(owner * out_w, 128), out_w)
        w_copies.append(pltpu.make_async_copy(w_hbm.at[:, columns], w_v.at[s], w_sem.at[s]))
    early = n_t // 2
    for copy in w_copies[:early]:
        copy.start()

    for r in range(reqs):
        slot_v[pl.ds(r, 1), :] = jnp.full((1, 128), slot_ref[id_ref[r]], jnp.int32)
    storage = slot_v[...]
    lane = lax.broadcasted_iota(jnp.int32, (reqs, 128), 1)
    holder = storage // residents
    local = storage - holder * residents
    local_hot = (local == lane).astype(F32).astype(BF16)
    away = holder - a
    away = jnp.where(away < 0, away + n_a, away)
    to_hot = away == lane
    before = lax.broadcasted_iota(jnp.int32, (reqs, reqs), 1) < lax.broadcasted_iota(
        jnp.int32, (reqs, reqs), 0
    )
    ranks = dot(before.astype(F32).astype(BF16), to_hot.astype(F32).astype(BF16))
    place = jnp.sum(jnp.where(to_hot, ranks, 0.0), axis=1, keepdims=True).astype(jnp.int32)
    place = place + away[:, :1] * cap
    packing = (
        (place == lax.broadcasted_iota(jnp.int32, (reqs, packed), 1)).astype(F32).astype(BF16)
    )

    for copy in small:
        copy.wait()
    for h in range(heads):
        qs[pl.ds(h, reqs, stride=heads), :] = q_v[
            :, h * HEAD_WIDTH : (h + 1) * HEAD_WIDTH
        ].astype(F32)
    kcf[...] = kc_v[...].astype(F32)
    vcf[...] = vc_v[...].astype(F32)

    def spread(block):
        return jnp.concatenate(
            [
                jnp.broadcast_to(
                    block[j : j + 1, c * HEAD_WIDTH : (c + 1) * HEAD_WIDTH], (per, HEAD_WIDTH)
                )
                for j in range(CHUNK)
                for c in range(kv)
            ],
            axis=0,
        )

    def attend(i, carry):
        k_copy, v_copy = cache_copies(i)
        rows = pl.ds(pl.multiple_of(i * (CHUNK * heads), CHUNK * heads), CHUNK * heads)
        part = pl.ds(pl.multiple_of(i * CHUNK, CHUNK), CHUNK)
        q_f = qs[rows, :]
        row_kv = lax.broadcasted_iota(jnp.int32, (heads, HEAD_WIDTH), 0) // per
        position = lax.broadcasted_iota(jnp.int32, (heads, span), 1)
        fresh = jnp.sum(q_f * spread(kcf[part, :]), axis=1, keepdims=True) * scaling
        k_copy.wait()
        scores = []
        for j in range(CHUNK):
            mine = q_f[j * heads : (j + 1) * heads]
            diag = jnp.concatenate(
                [jnp.where(row_kv == c, mine, 0.0) for c in range(kv)], axis=1
            ).astype(BF16)
            score = dot(diag, k_v[i * CHUNK + j], ((1,), (1,))) * scaling
            scores.append(jnp.where(position < len_ref[i * CHUNK + j], score, -jnp.inf))
        scores = jnp.concatenate(scores, axis=0)
        largest = jnp.maximum(jnp.max(scores, axis=1, keepdims=True), fresh)
        weights = jnp.exp(scores - largest)
        self_weight = jnp.exp(fresh - largest)
        total = jnp.sum(weights, axis=1, keepdims=True) + self_weight
        chances = (weights / total).astype(BF16)
        self_chance = (self_weight / total).astype(BF16).astype(F32)
        v_copy.wait()
        blended = []
        for j in range(CHUNK):
            both = dot(chances[j * heads : (j + 1) * heads], v_v[i * CHUNK + j])
            for c in range(kv):
                blended.append(
                    both[c * per : (c + 1) * per, c * HEAD_WIDTH : (c + 1) * HEAD_WIDTH]
                )
        blended = jnp.concatenate(blended, axis=0) + self_chance * spread(vcf[part, :])
        att[rows, :] = blended
        return carry

    lax.fori_loop(0, reqs // CHUNK, attend, 0)

    for h in range(heads):
        rows_a[:, h * HEAD_WIDTH : (h + 1) * HEAD_WIDTH] = att[
            pl.ds(h, reqs, stride=heads), :
        ].astype(BF16)

    pl.semaphore_wait(barrier, n_a - 1 + n_t - 1)

    step = 512
    for c in range(0, width, step):
        block = dot(packing, rows_a[:, c : c + step], ((0,), (0,))).astype(BF16)
        block = block.reshape(n_a, cap, step)
        row_send[:, :, c : c + step] = block
    row_send[:, :, width:] = (
        dot(packing, local_hot, ((0,), (0,))).astype(BF16).reshape(n_a, cap, 128)
    )
    row_copies = []
    for offset in range(1, n_a):
        copy = pltpu.make_async_remote_copy(
            src_ref=row_send.at[offset],
            dst_ref=row_recv.at[offset],
            send_sem=rs_sem.at[offset],
            recv_sem=rr_sem.at[offset],
            device_id=on_a(offset),
            device_id_type=MESH,
        )
        copy.start()
        row_copies.append(copy)
    for copy in w_copies[early:]:
        copy.start()
    down_copy.start()
    up_copy.start()

    part_copies = []

    def project(s, offset):
        w_copies[s].wait()
        half = out_w // 2
        for c in range(0, out_w, half):
            part_send[s, :, c : c + half] = dot(rows_a[...], w_v[s, :, c : c + half]).astype(BF16)
        copy = pltpu.make_async_remote_copy(
            src_ref=part_send.at[s],
            dst_ref=part_recv.at[s],
            send_sem=ps_sem.at[s],
            recv_sem=pr_sem.at[s],
            device_id=on_t(offset),
            device_id_type=MESH,
        )
        part_copies.append(copy)

    last = len(t_order) - 1
    for s, offset in enumerate(t_order):
        project(s, offset)
        if s < last - 1:
            part_copies[s].start()

    w_copies[n_t - 1].wait()
    share = dot(rows_a[...], w_v[n_t - 1])

    down_copy.wait()
    for copy in row_copies:
        copy.wait()
    got = jnp.concatenate([row_send[0][None], row_recv[1:]], axis=0).reshape(packed, width + 128)
    expand = (
        lax.broadcasted_iota(jnp.int32, (128, wide), 1) // rank
        == lax.broadcasted_iota(jnp.int32, (128, wide), 0)
    )
    chosen = dot(got[:, width:], expand.astype(F32).astype(BF16)) > 0.5
    low = dot(got[:, :width], down_v[...].reshape(wide, width), ((1,), (1,)))
    low = jnp.where(chosen, low, 0.0)
    fold = low[:, :128]
    for c in range(128, wide, 128):
        fold = fold + low[:, c : c + 128]
    fold = fold + pltpu.roll(fold, rank, 1)
    left = lax.broadcasted_iota(jnp.int32, (packed // 2, 128), 1) < rank
    own_low = jnp.where(left, fold[: packed // 2], fold[packed // 2 :])
    low_send[...] = own_low.astype(BF16)
    low_copies = []
    for offset in t_order:
        copy = pltpu.make_async_remote_copy(
            src_ref=low_send,
            dst_ref=low_recv.at[offset],
            send_sem=ls_sem.at[offset],
            recv_sem=lr_sem.at[offset],
            device_id=on_t(offset),
            device_id_type=MESH,
        )
        copy.start()
        low_copies.append(copy)
    part_copies[last - 1].start()
    part_copies[last].start()

    up_copy.wait()
    for copy in low_copies:
        copy.wait()
    for offset in t_order:
        own_low = own_low + low_recv[offset].astype(F32)
    turned = pltpu.roll(own_low, rank, 1)
    reduced = jnp.concatenate(
        [jnp.where(left, own_low, turned), jnp.where(left, turned, own_low)], axis=0
    )
    reduced = jnp.concatenate([reduced] * (wide // 128), axis=1)
    reduced = jnp.where(chosen, reduced, 0.0).astype(BF16)
    raised = dot(reduced, up_v[...].reshape(wide, out_w)).astype(BF16)
    back_send[...] = raised.reshape(n_a, cap, out_w)
    back_copies = []
    for offset in range(1, n_a):
        copy = pltpu.make_async_remote_copy(
            src_ref=back_send.at[offset],
            dst_ref=back_recv.at[offset],
            send_sem=bs_sem.at[offset],
            recv_sem=br_sem.at[offset],
            device_id=on_a(n_a - offset),
            device_id_type=MESH,
        )
        copy.start()
        back_copies.append(copy)

    for s, copy in enumerate(part_copies):
        copy.wait()
        share = share + part_recv[s].astype(F32)
    for copy in back_copies:
        copy.wait()
    came = jnp.concatenate([back_send[0][None], back_recv[1:]], axis=0).reshape(packed, out_w)
    out_ref[...] = (share + dot(packing, came)).astype(BF16)


def body(n_a, n_t, *operands):
    q, k, v, kc, vc, _, _, _, w, down, up = operands
    reqs, width = q.shape
    out_w = w.shape[1] // n_t
    cap = max(16, 2 * reqs // n_a)
    packed = n_a * cap
    heads = width // HEAD_WIDTH
    chunks = reqs // CHUNK
    dma = pltpu.SemaphoreType.DMA
    hbm = pl.BlockSpec(memory_space=pl.ANY)
    smem = pl.BlockSpec(memory_space=pltpu.SMEM)
    vmem = pltpu.VMEM
    return pl.pallas_call(
        functools.partial(kernel, n_a, n_t, cap),
        out_shape=jax.ShapeDtypeStruct((reqs, out_w), BF16),
        in_specs=[hbm] * 5 + [smem] * 3 + [hbm] * 3,
        out_specs=pl.BlockSpec(memory_space=pltpu.VMEM),
        scratch_shapes=[
            vmem(q.shape, BF16),
            vmem(k.shape, BF16),
            vmem(v.shape, BF16),
            vmem(kc.shape, BF16),
            vmem(vc.shape, BF16),
            vmem((n_t, width, out_w), BF16),
            vmem(down.shape, BF16),
            vmem(up.shape, BF16),
            vmem((reqs * heads, HEAD_WIDTH), F32),
            vmem((reqs * heads, HEAD_WIDTH), F32),
            vmem(kc.shape, F32),
            vmem(vc.shape, F32),
            vmem((reqs, 128), jnp.int32),
            vmem((reqs, width), BF16),
            vmem((n_t - 1, reqs, out_w), BF16),
            vmem((n_t - 1, reqs, out_w), BF16),
            vmem((n_a, cap, width + 128), BF16),
            vmem((n_a, cap, width + 128), BF16),
            vmem((packed // 2, 128), BF16),
            vmem((n_t, packed // 2, 128), BF16),
            vmem((n_a, cap, out_w), BF16),
            vmem((n_a, cap, out_w), BF16),
            dma((5,)),
            dma((chunks,)),
            dma((chunks,)),
            dma((n_t,)),
            dma((n_t,)),
            dma((n_t,)),
            dma((n_a,)),
            dma((n_a,)),
            dma((n_t,)),
            dma((n_t,)),
            dma((n_a,)),
            dma((n_a,)),
        ],
        compiler_params=pltpu.CompilerParams(
            collective_id=0, has_side_effects=True, vmem_limit_bytes=56 * 1024 * 1024
        ),
    )(*operands)


def solution(mesh):
    in_specs = (
        P(("groups", "adapter"), "tensor"),
        P(("groups", "adapter"), None, "tensor"),
        P(("groups", "adapter"), None, "tensor"),
        P(("groups", "adapter"), "tensor"),
        P(("groups", "adapter"), "tensor"),
        P(("groups", "adapter")),
        P(("groups", "adapter")),
        P("groups"),
        P("tensor", None),
        P("adapter", None, "tensor"),
        P("adapter", None, "tensor"),
    )
    out_specs = P(("groups", "adapter"), "tensor")
    run = functools.partial(body, mesh.shape["adapter"], mesh.shape["tensor"])
    return jax.shard_map(run, mesh=mesh, in_specs=in_specs, out_specs=out_specs, check_vma=False)
```

```python
import functools

import jax
import jax.numpy as jnp
from jax import lax
from jax.experimental import pallas as pl
from jax.experimental.pallas import tpu as pltpu
from jax.sharding import PartitionSpec as P

QUERY_HEADS = 64
KV_HEADS = 8
HEAD_WIDTH = 128
CHUNK = 32
MESH = pl.DeviceIdType.MESH
F32 = jnp.float32
BF16 = jnp.bfloat16


def offsets_of(n):
    return sorted(range(1, n), key=lambda o: (abs(o - n / 2), o))


def dot(a, b, dims=((1,), (0,))):
    return lax.dot_general(a, b, (dims, ((), ())), preferred_element_type=F32)


def kernel(
    n_a,
    n_t,
    cap,
    q_hbm,
    k_hbm,
    v_hbm,
    kc_hbm,
    vc_hbm,
    len_ref,
    id_ref,
    slot_ref,
    w_hbm,
    down_hbm,
    up_hbm,
    out_ref,
    q_v,
    k_v,
    v_v,
    kc_v,
    vc_v,
    w_v,
    down_v,
    up_v,
    qs,
    att,
    kcf,
    vcf,
    slot_v,
    rows_a,
    part_send,
    part_recv,
    row_send,
    row_recv,
    low_send,
    low_recv,
    back_send,
    back_recv,
    in_sem,
    k_sem,
    v_sem,
    w_sem,
    ps_sem,
    pr_sem,
    rs_sem,
    rr_sem,
    ls_sem,
    lr_sem,
    bs_sem,
    br_sem,
):
    g, a, t = lax.axis_index("groups"), lax.axis_index("adapter"), lax.axis_index("tensor")
    reqs, width = q_v.shape
    span = k_v.shape[1]
    heads = width // HEAD_WIDTH
    kv = kc_v.shape[1] // HEAD_WIDTH
    per = heads // kv
    residents, rank, _ = down_v.shape
    wide = residents * rank
    out_w = w_v.shape[2]
    packed = n_a * cap
    scaling = HEAD_WIDTH ** (-0.5)
    t_order = offsets_of(n_t)

    def on_t(offset):
        return (g, a, lax.rem(t + offset, n_t))

    def on_a(offset):
        return (g, lax.rem(a + offset, n_a), t)

    barrier = pltpu.get_barrier_semaphore()
    for offset in range(1, n_a):
        pl.semaphore_signal(barrier, inc=1, device_id=on_a(offset), device_id_type=MESH)
    for offset in range(1, n_t):
        pl.semaphore_signal(barrier, inc=1, device_id=on_t(offset), device_id_type=MESH)

    small = [
        pltpu.make_async_copy(q_hbm, q_v, in_sem.at[0]),
        pltpu.make_async_copy(kc_hbm, kc_v, in_sem.at[1]),
        pltpu.make_async_copy(vc_hbm, vc_v, in_sem.at[2]),
    ]
    down_copy = pltpu.make_async_copy(down_hbm, down_v, in_sem.at[3])
    up_copy = pltpu.make_async_copy(up_hbm, up_v, in_sem.at[4])

    def cache_copies(i):
        part = pl.ds(pl.multiple_of(i * CHUNK, CHUNK), CHUNK)
        return (
            pltpu.make_async_copy(k_hbm.at[part], k_v.at[part], k_sem.at[i]),
            pltpu.make_async_copy(v_hbm.at[part], v_v.at[part], v_sem.at[i]),
        )

    for copy in small:
        copy.start()
    for i in range(reqs // CHUNK):
        for copy in cache_copies(i):
            copy.start()
    w_copies = []
    for s, offset in enumerate(t_order + [0]):
        owner = lax.rem(t + offset, n_t)
        columns = pl.ds(pl.multiple_of(owner * out_w, 128), out_w)
        w_copies.append(pltpu.make_async_copy(w_hbm.at[:, columns], w_v.at[s], w_sem.at[s]))
    early = 1
    for copy in w_copies[:early]:
        copy.start()

    for r in range(reqs):
        slot_v[pl.ds(r, 1), :] = jnp.full((1, 128), slot_ref[id_ref[r]], jnp.int32)
    storage = slot_v[...]
    lane = lax.broadcasted_iota(jnp.int32, (reqs, 128), 1)
    holder = storage // residents
    local = storage - holder * residents
    local_hot = (local == lane).astype(F32).astype(BF16)
    away = holder - a
    away = jnp.where(away < 0, away + n_a, away)
    to_hot = away == lane
    before = lax.broadcasted_iota(jnp.int32, (reqs, reqs), 1) < lax.broadcasted_iota(
        jnp.int32, (reqs, reqs), 0
    )
    ranks = dot(before.astype(F32).astype(BF16), to_hot.astype(F32).astype(BF16))
    place = jnp.sum(jnp.where(to_hot, ranks, 0.0), axis=1, keepdims=True).astype(jnp.int32)
    place = place + away[:, :1] * cap
    packing = (
        (place == lax.broadcasted_iota(jnp.int32, (reqs, packed), 1)).astype(F32).astype(BF16)
    )

    for copy in small:
        copy.wait()
    for h in range(heads):
        qs[pl.ds(h, reqs, stride=heads), :] = q_v[
            :, h * HEAD_WIDTH : (h + 1) * HEAD_WIDTH
        ].astype(F32)
    kcf[...] = kc_v[...].astype(F32)
    vcf[...] = vc_v[...].astype(F32)

    def spread(block):
        return jnp.concatenate(
            [
                jnp.broadcast_to(
                    block[j : j + 1, c * HEAD_WIDTH : (c + 1) * HEAD_WIDTH], (per, HEAD_WIDTH)
                )
                for j in range(CHUNK)
                for c in range(kv)
            ],
            axis=0,
        )

    def attend(i, carry):
        k_copy, v_copy = cache_copies(i)
        rows = pl.ds(pl.multiple_of(i * (CHUNK * heads), CHUNK * heads), CHUNK * heads)
        part = pl.ds(pl.multiple_of(i * CHUNK, CHUNK), CHUNK)
        q_f = qs[rows, :]
        row_kv = lax.broadcasted_iota(jnp.int32, (heads, HEAD_WIDTH), 0) // per
        position = lax.broadcasted_iota(jnp.int32, (heads, span), 1)
        fresh = jnp.sum(q_f * spread(kcf[part, :]), axis=1, keepdims=True) * scaling
        k_copy.wait()
        scores = []
        for j in range(CHUNK):
            mine = q_f[j * heads : (j + 1) * heads]
            diag = jnp.concatenate(
                [jnp.where(row_kv == c, mine, 0.0) for c in range(kv)], axis=1
            ).astype(BF16)
            score = dot(diag, k_v[i * CHUNK + j], ((1,), (1,))) * scaling
            scores.append(jnp.where(position < len_ref[i * CHUNK + j], score, -jnp.inf))
        scores = jnp.concatenate(scores, axis=0)
        largest = jnp.maximum(jnp.max(scores, axis=1, keepdims=True), fresh)
        weights = jnp.exp(scores - largest)
        self_weight = jnp.exp(fresh - largest)
        total = jnp.sum(weights, axis=1, keepdims=True) + self_weight
        chances = (weights / total).astype(BF16)
        self_chance = (self_weight / total).astype(BF16).astype(F32)
        v_copy.wait()
        blended = []
        for j in range(CHUNK):
            both = dot(chances[j * heads : (j + 1) * heads], v_v[i * CHUNK + j])
            for c in range(kv):
                blended.append(
                    both[c * per : (c + 1) * per, c * HEAD_WIDTH : (c + 1) * HEAD_WIDTH]
                )
        blended = jnp.concatenate(blended, axis=0) + self_chance * spread(vcf[part, :])
        att[rows, :] = blended
        return carry

    lax.fori_loop(0, reqs // CHUNK, attend, 0)

    for h in range(heads):
        rows_a[:, h * HEAD_WIDTH : (h + 1) * HEAD_WIDTH] = att[
            pl.ds(h, reqs, stride=heads), :
        ].astype(BF16)

    pl.semaphore_wait(barrier, n_a - 1 + n_t - 1)

    step = 512
    for c in range(0, width, step):
        block = dot(packing, rows_a[:, c : c + step], ((0,), (0,))).astype(BF16)
        block = block.reshape(n_a, cap, step)
        row_send[:, :, c : c + step] = block
    row_send[:, :, width:] = (
        dot(packing, local_hot, ((0,), (0,))).astype(BF16).reshape(n_a, cap, 128)
    )
    row_copies = []
    for offset in range(1, n_a):
        copy = pltpu.make_async_remote_copy(
            src_ref=row_send.at[offset],
            dst_ref=row_recv.at[offset],
            send_sem=rs_sem.at[offset],
            recv_sem=rr_sem.at[offset],
            device_id=on_a(offset),
            device_id_type=MESH,
        )
        copy.start()
        row_copies.append(copy)
    for copy in w_copies[early:]:
        copy.start()
    down_copy.start()
    up_copy.start()

    part_copies = []

    def project(s, offset):
        w_copies[s].wait()
        half = out_w // 2
        for c in range(0, out_w, half):
            part_send[s, :, c : c + half] = dot(rows_a[...], w_v[s, :, c : c + half]).astype(BF16)
        copy = pltpu.make_async_remote_copy(
            src_ref=part_send.at[s],
            dst_ref=part_recv.at[s],
            send_sem=ps_sem.at[s],
            recv_sem=pr_sem.at[s],
            device_id=on_t(offset),
            device_id_type=MESH,
        )
        part_copies.append(copy)

    last = len(t_order) - 1
    for s, offset in enumerate(t_order):
        project(s, offset)
        if s < last - 1:
            part_copies[s].start()

    w_copies[n_t - 1].wait()
    share = dot(rows_a[...], w_v[n_t - 1])

    down_copy.wait()
    for copy in row_copies:
        copy.wait()
    got = jnp.concatenate([row_send[0][None], row_recv[1:]], axis=0).reshape(packed, width + 128)
    expand = (
        lax.broadcasted_iota(jnp.int32, (128, wide), 1) // rank
        == lax.broadcasted_iota(jnp.int32, (128, wide), 0)
    )
    chosen = dot(got[:, width:], expand.astype(F32).astype(BF16)) > 0.5
    low = dot(got[:, :width], down_v[...].reshape(wide, width), ((1,), (1,)))
    low = jnp.where(chosen, low, 0.0)
    fold = low[:, :128]
    for c in range(128, wide, 128):
        fold = fold + low[:, c : c + 128]
    fold = fold + pltpu.roll(fold, rank, 1)
    left = lax.broadcasted_iota(jnp.int32, (packed // 2, 128), 1) < rank
    own_low = jnp.where(left, fold[: packed // 2], fold[packed // 2 :])
    low_send[...] = own_low.astype(BF16)
    low_copies = []
    for offset in t_order:
        copy = pltpu.make_async_remote_copy(
            src_ref=low_send,
            dst_ref=low_recv.at[offset],
            send_sem=ls_sem.at[offset],
            recv_sem=lr_sem.at[offset],
            device_id=on_t(offset),
            device_id_type=MESH,
        )
        copy.start()
        low_copies.append(copy)
    part_copies[last - 1].start()
    part_copies[last].start()

    up_copy.wait()
    for copy in low_copies:
        copy.wait()
    for offset in t_order:
        own_low = own_low + low_recv[offset].astype(F32)
    turned = pltpu.roll(own_low, rank, 1)
    reduced = jnp.concatenate(
        [jnp.where(left, own_low, turned), jnp.where(left, turned, own_low)], axis=0
    )
    reduced = jnp.concatenate([reduced] * (wide // 128), axis=1)
    reduced = jnp.where(chosen, reduced, 0.0).astype(BF16)
    raised = dot(reduced, up_v[...].reshape(wide, out_w)).astype(BF16)
    back_send[...] = raised.reshape(n_a, cap, out_w)
    back_copies = []
    for offset in range(1, n_a):
        copy = pltpu.make_async_remote_copy(
            src_ref=back_send.at[offset],
            dst_ref=back_recv.at[offset],
            send_sem=bs_sem.at[offset],
            recv_sem=br_sem.at[offset],
            device_id=on_a(n_a - offset),
            device_id_type=MESH,
        )
        copy.start()
        back_copies.append(copy)

    for s, copy in enumerate(part_copies):
        copy.wait()
        share = share + part_recv[s].astype(F32)
    for copy in back_copies:
        copy.wait()
    came = jnp.concatenate([back_send[0][None], back_recv[1:]], axis=0).reshape(packed, out_w)
    out_ref[...] = (share + dot(packing, came)).astype(BF16)


def body(n_a, n_t, *operands):
    q, k, v, kc, vc, _, _, _, w, down, up = operands
    reqs, width = q.shape
    out_w = w.shape[1] // n_t
    cap = max(16, 2 * reqs // n_a)
    packed = n_a * cap
    heads = width // HEAD_WIDTH
    chunks = reqs // CHUNK
    dma = pltpu.SemaphoreType.DMA
    hbm = pl.BlockSpec(memory_space=pl.ANY)
    smem = pl.BlockSpec(memory_space=pltpu.SMEM)
    vmem = pltpu.VMEM
    return pl.pallas_call(
        functools.partial(kernel, n_a, n_t, cap),
        out_shape=jax.ShapeDtypeStruct((reqs, out_w), BF16),
        in_specs=[hbm] * 5 + [smem] * 3 + [hbm] * 3,
        out_specs=pl.BlockSpec(memory_space=pltpu.VMEM),
        scratch_shapes=[
            vmem(q.shape, BF16),
            vmem(k.shape, BF16),
            vmem(v.shape, BF16),
            vmem(kc.shape, BF16),
            vmem(vc.shape, BF16),
            vmem((n_t, width, out_w), BF16),
            vmem(down.shape, BF16),
            vmem(up.shape, BF16),
            vmem((reqs * heads, HEAD_WIDTH), F32),
            vmem((reqs * heads, HEAD_WIDTH), F32),
            vmem(kc.shape, F32),
            vmem(vc.shape, F32),
            vmem((reqs, 128), jnp.int32),
            vmem((reqs, width), BF16),
            vmem((n_t - 1, reqs, out_w), BF16),
            vmem((n_t - 1, reqs, out_w), BF16),
            vmem((n_a, cap, width + 128), BF16),
            vmem((n_a, cap, width + 128), BF16),
            vmem((packed // 2, 128), BF16),
            vmem((n_t, packed // 2, 128), BF16),
            vmem((n_a, cap, out_w), BF16),
            vmem((n_a, cap, out_w), BF16),
            dma((5,)),
            dma((chunks,)),
            dma((chunks,)),
            dma((n_t,)),
            dma((n_t,)),
            dma((n_t,)),
            dma((n_a,)),
            dma((n_a,)),
            dma((n_t,)),
            dma((n_t,)),
            dma((n_a,)),
            dma((n_a,)),
        ],
        compiler_params=pltpu.CompilerParams(
            collective_id=0, has_side_effects=True, vmem_limit_bytes=56 * 1024 * 1024
        ),
    )(*operands)


def solution(mesh):
    in_specs = (
        P(("groups", "adapter"), "tensor"),
        P(("groups", "adapter"), None, "tensor"),
        P(("groups", "adapter"), None, "tensor"),
        P(("groups", "adapter"), "tensor"),
        P(("groups", "adapter"), "tensor"),
        P(("groups", "adapter")),
        P(("groups", "adapter")),
        P("groups"),
        P("tensor", None),
        P("adapter", None, "tensor"),
        P("adapter", None, "tensor"),
    )
    out_specs = P(("groups", "adapter"), "tensor")
    run = functools.partial(body, mesh.shape["adapter"], mesh.shape["tensor"])
    return jax.shard_map(run, mesh=mesh, in_specs=in_specs, out_specs=out_specs, check_vma=False)
```
